256 devices in a mesh: dom: 4 (over x), dp: 64 (over z, y, core).
Axes of the slice: x: 4, y: 4, z: 8, core: 2. Of those that a mesh axis runs over, the one named last changes fastest.
Arguments:
- records: bfloat16 [131072, 2048], P('dp'), may hold values from -6 to 6
- counts_obs: int32 [131072], P('dp'), may hold values from 0 to 7
- exposure_bin: int32 [131072], P('dp'), may hold values from 0 to 63
- bin_offset: float32 [64], replicated, may hold values from -1.5 to 0.5
- theta: float32 [2048, 2048], P('dom', 'dp'), may hold values from -6 to 6
- noise: float32 [2048, 2048], P('dom', 'dp'), may hold values from -6 to 6
- offspring: int32 [2048], replicated, may hold values from 0 to 16, as said below
- slot_order: int32 [2048], replicated, may hold values from 0 to 2047, each once
- temper_step: float32 [], replicated, may hold values from 0.0069053397 to 0.013810679
- temper_level: float32 [], replicated, may hold values from 0.5 to 2
- step_size: float32 [], replicated, may hold values from 0.02 to 0.1
Outputs:
- moved: float32 [2048, 2048], P('dom', 'dp')
- log_evidence: float32 [], replicated
- ess_fraction: float32 [], replicated
The draws below stay inside these ranges and needn't reach their ends.
Inputs may be any that keep to these rules, and one draw needn't show every extreme that they name: The counts sum to 2048: 32 particles have 16 offspring, half of the particles one, an eighth two, the rest none, placed in random order. `slot_order`: each slot appears once.
All inputs are finite; a program needn't handle non-finite values.
Results may differ from the reference program's by a relative error of at most 0.0028.
The reference program's roundings to bfloat16 on the way (of `theta_low` and `residual`) count: a program that leaves them out, or rounds other values in their place, can miss the bound.
Values may be sent and summed in bfloat16 or wider, within the bound.
A program may use at most 64 MiB of HBM per device.

```python
import math
import jax
import jax.numpy as jnp
from jax import lax

D = 2048
NBINS = 64
MOST = 16
ROWS_DEV = 2048
RECORDS = 131072
P_SIZE = 2048
N_DP = 64


def draw_offspring(key, part):
    key = jax.random.fold_in(key, 11)
    ranking = jax.random.permutation(key, P_SIZE)
    heavy_end = P_SIZE // (4 * MOST)
    single_end = heavy_end + P_SIZE // 2
    double_end = single_end + P_SIZE // 8
    counts = jnp.where(ranking < heavy_end, MOST, jnp.where(ranking < single_end, 1, jnp.where(ranking < double_end, 2, 0)))
    return counts.astype(jnp.int32)


def plant(values, stream_key, smallest, top_value):
    index_at = [jax.random.randint(jax.random.fold_in(stream_key, axis), (), 0, length) for axis, length in enumerate(values.shape)]
    widest = values.shape.index(max(values.shape))
    beside = index_at[:widest] + [(index_at[widest] + 1) % values.shape[widest]] + index_at[widest + 1:]
    return values.at[tuple(index_at)].set(smallest).at[tuple(beside)].set(top_value)


def levels(own_key, extent, pieces, smallest, top_value):
    def one(axis_at, blocks):
        heights = jax.random.uniform(jax.random.fold_in(jax.random.fold_in(own_key, 6), axis_at), (blocks,), jnp.float32, smallest / len(pieces), top_value / len(pieces))
        return jnp.repeat(jnp.exp(heights), extent[axis_at] // blocks).reshape((-1,) + (1,) * (len(extent) - axis_at - 1))

    factor_of = one(*pieces[0])
    for cut in pieces[1:]:
        factor_of = factor_of * one(*cut)
    return factor_of


def centred(rng, extent, width, most, pieces=(), held_as=jnp.bfloat16):
    level = levels(rng, extent, pieces, -0.22, 0.18) if pieces else 1.0
    drawn = jax.random.normal(rng, extent, jnp.float32) * width * level
    return jnp.minimum(jnp.maximum(drawn, -most), most).astype(held_as)


def setup_inputs(seed: int = 0) -> dict:
    arg_keys = jax.random.split(jax.random.key(seed), 12)
    records = centred(arg_keys[0], (RECORDS, D), 1.0, 6.0, ((0, 64),))
    counts_obs = plant(jax.random.randint(arg_keys[1], (RECORDS,), 0, 8), jax.random.fold_in(arg_keys[1], 1), 0, 7).astype(jnp.int32)
    exposure_bin = plant(jax.random.randint(arg_keys[2], (RECORDS,), 0, NBINS), jax.random.fold_in(arg_keys[2], 1), 0, NBINS - 1).astype(jnp.int32)
    bin_offset = jnp.clip(jax.random.uniform(arg_keys[3], (NBINS,), jnp.float32, -1.5, 0.5), -1.5, 0.5)
    theta = centred(arg_keys[4], (P_SIZE, D), 1.0, 6.0, ((0, 4), (1, 64)), jnp.float32)
    noise = centred(arg_keys[5], (P_SIZE, D), 1.0, 6.0, ((0, 4), (1, 64)), jnp.float32)
    offspring = draw_offspring(jax.random.fold_in(arg_keys[11], 71), 0)
    slot_order = jax.random.permutation(arg_keys[7], P_SIZE).astype(jnp.int32)
    temper_step = jnp.clip(jnp.exp(jax.random.uniform(arg_keys[8], (), jnp.float32, math.log(0.0069053397), math.log(0.013810679))), 0.0069053397, 0.013810679)
    temper_level = jnp.clip(jnp.exp(jax.random.uniform(arg_keys[9], (), jnp.float32, math.log(0.5), math.log(2.0))), 0.5, 2.0)
    step_size = jnp.clip(jnp.exp(jax.random.uniform(arg_keys[10], (), jnp.float32, math.log(0.02), math.log(0.1))), 0.02, 0.1)
    return {"records": records, "counts_obs": counts_obs, "exposure_bin": exposure_bin, "bin_offset": bin_offset, "theta": theta, "noise": noise, "offspring": offspring, "slot_order": slot_order, "temper_step": temper_step, "temper_level": temper_level, "step_size": step_size}


def reference(records, counts_obs, exposure_bin, bin_offset, theta, noise, offspring, slot_order, temper_step, temper_level, step_size):
    scale_in = 1.0 / math.sqrt(D)
    temper_scale = math.sqrt(D / RECORDS)
    theta_low = theta.astype(jnp.bfloat16)
    offset = bin_offset[exposure_bin]
    target = counts_obs.astype(jnp.float32)
    log_factorial = jax.scipy.special.gammaln(target + 1.0)
    record_blocks = records.reshape(N_DP, ROWS_DEV, D)
    offset_blocks = offset.reshape(N_DP, ROWS_DEV)
    target_blocks = target.reshape(N_DP, ROWS_DEV)
    factorial_blocks = log_factorial.reshape(N_DP, ROWS_DEV)

    def accumulate(running, entries):
        block_rows, block_offset, block_target, block_factorial = entries
        linear = jnp.dot(block_rows, theta_low.T, preferred_element_type=jnp.float32) * scale_in + block_offset[:, None]
        intensity = jnp.exp(linear)
        loglik = running[0] + lax.optimization_barrier(jnp.sum(block_target[:, None] * linear - intensity, axis=0)) - jnp.sum(block_factorial)
        residual = (block_target[:, None] - intensity).astype(jnp.bfloat16)
        score = running[1] + jnp.dot(residual.T, block_rows, preferred_element_type=jnp.float32)
        return ((loglik, score), None)
    start_state = (jnp.zeros((P_SIZE,), jnp.float32), jnp.zeros((P_SIZE, D), jnp.float32))
    (loglik, score), _ = lax.scan(accumulate, start_state, (record_blocks, offset_blocks, target_blocks, factorial_blocks))
    log_weight = temper_step * temper_scale * loglik
    peak_value = jnp.max(log_weight)
    shifted = jnp.exp(log_weight - peak_value)
    weight_sum = jnp.sum(shifted)
    weight_square = jnp.sum(shifted * shifted)
    log_evidence = peak_value + jnp.log(weight_sum) - math.log(P_SIZE)
    ess_fraction = weight_sum * weight_sum / (weight_square * P_SIZE)
    drift_term = -theta + temper_level * (temper_scale * scale_in) * score
    cumulative = jnp.cumsum(offspring).astype(jnp.int32)
    ancestor = jnp.searchsorted(cumulative, slot_order.astype(jnp.int32), side='right').astype(jnp.int32)
    moved = theta[ancestor] + 0.5 * step_size * drift_term[ancestor] + jnp.sqrt(step_size) * noise
    return (moved, log_evidence, ess_fraction)
```

```python
import functools
import math

import jax
import jax.numpy as jnp
from jax import lax
from jax.experimental import pallas as pl
from jax.experimental.pallas import tpu as pltpu
from jax.sharding import PartitionSpec as P

F32, BF16 = jnp.float32, jnp.bfloat16
MESH = pl.DeviceIdType.MESH
NZ, NY, NX = 8, 4, 4
Z_ORDER = (4, 3, 5, 2, 6, 1, 7)
Z_ARRIVE = (1, 7, 2, 6, 3, 5, 4)
Y_STEPS = (2, 1, 3, 0)


def kernel(
    rec_hbm, cnt_ref, bin_ref, bo_ref, th_ref, nz_ref, offs_ref, slot_ref, tstep_ref, tlev_ref, step_ref,
    out_ref, le_ref, ess_ref,
    rec, rect, thg, res, offb, cntb, sel, thx, base, scf, snd_c, rcv_c, snd_y, rcv_y, snd_z, rcv_z, scx,
    ll_own, ll_c, ll_y, ll_z, ll_x,
    rec_sem, gz_s, gz_r, gy_s, gy_r, gc_s, gc_r, tx_s, tx_r, c_s, c_r, y_s, y_r, z_s, z_r, x_s, x_r,
    lc_s, lc_r, ly_s, ly_r, lz_s, lz_r, lx_s, lx_r,
):
    x = lax.axis_index("dom")
    dp = lax.axis_index("dp")
    z, y, c = dp // 8, (dp // 2) % 4, dp % 2
    n_rec, n_feat = rec.shape
    n_part = th_ref.shape[1]
    scale_in = 1.0 / math.sqrt(n_feat)
    temper_scale = math.sqrt(n_feat / (n_rec * NZ * NY * 2))

    def at(zz, yy, cc):
        return (x, zz * 8 + yy * 2 + cc)

    sib = at(z, y, 1 - c)
    zs = [lax.rem(z + k, NZ) for k in range(NZ)]
    ys = [lax.rem(y + k, NY) for k in range(NY)]
    xs = [lax.rem(x + k, NX) for k in range(NX)]

    barrier = pltpu.get_barrier_semaphore()
    peers = [sib] + [at(zs[k], y, c) for k in Z_ORDER] + [at(z, ys[k], c) for k in (2, 1, 3)] + [(xs[k], dp) for k in (2, 1, 3)]
    for peer in peers:
        pl.semaphore_signal(barrier, inc=1, device_id=peer, device_id_type=MESH)

    blk = n_rec // 8
    loads = []
    for i in range(8):
        cp = pltpu.make_async_copy(rec_hbm.at[pl.ds(i * blk, blk)], rec.at[pl.ds(i * blk, blk)], rec_sem.at[i])
        cp.start()
        loads.append(cp)

    theta = th_ref[...]
    thg[z, y, c] = theta.astype(BF16)
    thx[x] = theta

    pl.semaphore_wait(barrier, len(peers))

    sends = []

    def send(src, dst, ss, rs, dev):
        cp = pltpu.make_async_remote_copy(src_ref=src, dst_ref=dst, send_sem=ss, recv_sem=rs, device_id=dev, device_id_type=MESH)
        cp.start()
        sends.append(cp)

    def arrived(dst, rs):
        pltpu.make_async_remote_copy(src_ref=dst, dst_ref=dst, send_sem=rs, recv_sem=rs, device_id=sib, device_id_type=MESH).wait_recv()

    own = thg.at[z, y, c]
    for k in Z_ORDER:
        send(own, own, gz_s.at[k], gz_r.at[k], at(zs[k], y, c))

    def to_y(k):
        part = thg.at[lax.rem(z + NZ - k, NZ), y, c]
        for j in (2, 1, 3):
            send(part, part, gy_s.at[j, k], gy_r.at[j, k], at(z, ys[j], c))

    to_y(0)
    for k in (2, 1, 3):
        send(thx.at[x], thx.at[x], tx_s.at[k], tx_r.at[k], (xs[k], dp))

    bins = bin_ref[...]
    off = jnp.zeros(bins.shape, F32)
    for b in range(bo_ref.shape[0]):
        off = jnp.where(bins == b, bo_ref[b], off)
    counts = cnt_ref[...]
    table = jnp.zeros(counts.shape, F32)
    for n in range(2, 8):
        table = jnp.where(counts == n, math.lgamma(n + 1.0), table)
    log_factorial = jnp.sum(table)
    cntf = counts.astype(F32)
    for i in range(n_rec // 128):
        rows = pl.ds(128 * i, 128)
        offb[rows, :] = jnp.broadcast_to(off[i : i + 1, :], (128, 128)).T
        cntb[rows, :] = jnp.broadcast_to(cntf[i : i + 1, :], (128, 128)).T

    def transpose_block(i):
        loads[i].wait()
        rect[:, :, :, pl.ds(i * blk, blk)] = rec[pl.ds(i * blk, blk), :].T.reshape(NZ, NY, 64, blk)

    for i, k in enumerate(Z_ARRIVE):
        arrived(thg.at[lax.rem(z + NZ - k, NZ), y, c], gz_r.at[k])
        to_y(k)
        transpose_block(i)
    send(thg.at[:, y, c], thg.at[:, y, c], gc_s.at[0], gc_r.at[0], sib)
    transpose_block(7)

    offs = offs_ref[...].astype(F32)
    upper = (lax.broadcasted_iota(jnp.int32, (128, 128), 0) <= lax.broadcasted_iota(jnp.int32, (128, 128), 1)).astype(F32).astype(BF16)
    within = jnp.dot(offs.astype(BF16), upper, preferred_element_type=F32)
    slots = jnp.concatenate([slot_ref[pl.ds(x * 4 + q, 1), :] for q in range(4)], axis=1).astype(F32)
    before = jnp.zeros((1, 1), F32)
    for i in range(offs.shape[0]):
        upto = within[i : i + 1, :] + before
        start = upto - offs[i : i + 1, :]
        upto_b = jnp.broadcast_to(upto, (128, 128)).T
        start_b = jnp.broadcast_to(start, (128, 128)).T
        for q in range(4):
            lanes = slice(128 * q, 128 * q + 128)
            hit = (slots[:, lanes] >= start_b) & (slots[:, lanes] < upto_b)
            sel[128 * i : 128 * i + 128, lanes] = jnp.where(hit, 1.0, 0.0).astype(BF16)
        before = before + within[i : i + 1, 127:128]

    for j in (1, 3, 2):
        yy = lax.rem(y + NY - j, NY)
        for k in range(NZ):
            arrived(thg.at[lax.rem(z + NZ - k, NZ), yy, c], gy_r.at[j, k])
        send(thg.at[:, yy, c], thg.at[:, yy, c], gc_s.at[j], gc_r.at[j], sib)
    for j in (0, 1, 3, 2):
        yy = lax.rem(y + NY - j, NY)
        arrived(thg.at[:, yy, 1 - c], gc_r.at[j])

    ll_own[...] = jnp.full(ll_own.shape, -log_factorial / 8.0, F32)

    @pl.loop(0, n_rec // 512)
    def _(i):
        rows = pl.ds(pl.multiple_of(i * 512, 512), 512)
        prod = jnp.dot(rec[rows, :], thg[...].reshape(n_feat, n_part), preferred_element_type=F32)
        o, t = offb[rows, :], cntb[rows, :]
        for q in range(n_part // 128):
            lanes = slice(128 * q, 128 * q + 128)
            lin = prod[:, lanes] * scale_in + o
            inten = jnp.exp(lin)
            ll_own[:, lanes] += jnp.sum((t * lin - inten).reshape(64, 8, 128), axis=0)
            res[rows, lanes] = (t - inten).astype(BF16)

    send(ll_own, ll_c, lc_s, lc_r, sib)

    def after_c(s):
        j = Y_STEPS[s]
        arrived(rcv_c.at[s], c_r.at[s])
        total = scf[s, :, c] + rcv_c[s].astype(F32)
        if j == 0:
            return total
        snd_y[s] = total.astype(BF16)
        send(snd_y.at[s], rcv_y.at[s], y_s.at[s], y_r.at[s], at(z, ys[j], c))

    for s, j in enumerate(Y_STEPS):
        part = jnp.dot(rect[:, ys[j]].reshape(512, n_rec), res[...], preferred_element_type=F32)
        scf[s] = part.reshape(NZ, 2, 32, n_part)
        snd_c[s] = scf[s, :, 1 - c].astype(BF16)
        send(snd_c.at[s], rcv_c.at[s], c_s.at[s], c_r.at[s], sib)
        if s == 0:
            arrived(ll_c, lc_r)
            ll_y[y] = ll_own[...] + ll_c[...]
            for k in (2, 1, 3):
                send(ll_y.at[y], ll_y.at[y], ly_s.at[k], ly_r.at[k], at(z, ys[k], c))
        else:
            after_c(s - 1)
    for k in (1, 3, 2):
        arrived(ll_y.at[lax.rem(y + NY - k, NY)], ly_r.at[k])
    ll_z[z] = (ll_y[0] + ll_y[1]) + (ll_y[2] + ll_y[3])
    for k in Z_ORDER:
        send(ll_z.at[z], ll_z.at[z], lz_s.at[k], lz_r.at[k], at(zs[k], y, c))
    total = after_c(3)
    for s in range(3):
        arrived(rcv_y.at[s], y_r.at[s])
        total = total + rcv_y[s].astype(F32)
    scf[0, :, 0] = total
    snd_z[...] = total.astype(BF16)
    for k in Z_ORDER:
        send(snd_z.at[zs[k]], rcv_z.at[k], z_s.at[k], z_r.at[k], at(zs[k], y, c))

    for k in (1, 3, 2):
        arrived(thx.at[lax.rem(x + NX - k, NX)], tx_r.at[k])
    everyone = jnp.concatenate([thx[q] for q in range(NX)], axis=1)
    hi = everyone.astype(BF16)
    rest = everyone - hi.astype(F32)
    mid = rest.astype(BF16)
    lo = (rest - mid.astype(F32)).astype(BF16)
    taken = jnp.dot(jnp.concatenate([hi, mid, lo], axis=0), sel[...], preferred_element_type=F32)
    taken = taken[0:32] + taken[32:64] + taken[64:96]
    step = step_ref[0]
    root = jnp.sqrt(jnp.full((1, 1), step, F32))
    base[...] = (1.0 - 0.5 * step) * taken + root * nz_ref[...]

    for k in Z_ARRIVE:
        arrived(ll_z.at[lax.rem(z + NZ - k, NZ)], lz_r.at[k])
    ll_x[x] = ((ll_z[0] + ll_z[1]) + (ll_z[2] + ll_z[3])) + ((ll_z[4] + ll_z[5]) + (ll_z[6] + ll_z[7]))
    for k in (2, 1, 3):
        send(ll_x.at[x], ll_x.at[x], lx_s.at[k], lx_r.at[k], (xs[k], dp))

    score = scf[0, z, 0]
    for k in Z_ARRIVE:
        arrived(rcv_z.at[k], z_r.at[k])
        score = score + rcv_z[k].astype(F32)
    scx[x] = score.astype(BF16)
    for k in (2, 1, 3):
        send(scx.at[x], scx.at[x], x_s.at[k], x_r.at[k], (xs[k], dp))

    for k in (1, 3, 2):
        arrived(ll_x.at[lax.rem(x + NX - k, NX)], lx_r.at[k])
    loglik = jnp.concatenate([jnp.sum(ll_x[q], axis=0, keepdims=True) for q in range(NX)], axis=0)
    log_weight = tstep_ref[0] * temper_scale * loglik
    peak = jnp.max(log_weight, axis=(0, 1), keepdims=True)
    shifted = jnp.exp(log_weight - peak)
    weight_sum = jnp.sum(shifted, axis=(0, 1), keepdims=True)
    weight_square = jnp.sum(shifted * shifted, axis=(0, 1), keepdims=True)
    le_ref[...] = peak + jnp.log(weight_sum) - math.log(NX * n_part)
    ess_ref[...] = weight_sum * weight_sum / (weight_square * (NX * n_part))

    for k in (1, 3, 2):
        arrived(scx.at[lax.rem(x + NX - k, NX)], x_r.at[k])
    scores = jnp.concatenate([scx[q] for q in range(NX)], axis=1)
    taken = jnp.dot(scores, sel[...], preferred_element_type=F32)
    out_ref[...] = base[...] + (0.5 * step * tlev_ref[0] * (temper_scale * scale_in)) * taken

    for cp in sends:
        cp.wait_send()


def on_device(records, counts_obs, exposure_bin, bin_offset, theta, noise, offspring, slot_order, temper_step, temper_level, step_size):
    n_rec, n_feat = records.shape
    n_part, cols = theta.shape
    vmem, smem = pl.BlockSpec(memory_space=pltpu.VMEM), pl.BlockSpec(memory_space=pltpu.SMEM)
    dma = pltpu.SemaphoreType.DMA
    blocks = (NZ, cols, n_part)
    scratch = [
        pltpu.VMEM((n_rec, n_feat), BF16),
        pltpu.VMEM((NZ, NY, 64, n_rec), BF16),
        pltpu.VMEM((NZ, NY, 2, cols, n_part), BF16),
        pltpu.VMEM((n_rec, n_part), BF16),
        pltpu.VMEM((n_rec, 128), F32),
        pltpu.VMEM((n_rec, 128), F32),
        pltpu.VMEM((NX * n_part, n_part), BF16),
        pltpu.VMEM((NX, cols, n_part), F32),
        pltpu.VMEM((cols, n_part), F32),
        pltpu.VMEM((4, NZ, 2, cols, n_part), F32),
        pltpu.VMEM((4,) + blocks, BF16),
        pltpu.VMEM((4,) + blocks, BF16),
        pltpu.VMEM((3,) + blocks, BF16),
        pltpu.VMEM((3,) + blocks, BF16),
        pltpu.VMEM(blocks, BF16),
        pltpu.VMEM(blocks, BF16),
        pltpu.VMEM((NX, cols, n_part), BF16),
        pltpu.VMEM((8, n_part), F32),
        pltpu.VMEM((8, n_part), F32),
        pltpu.VMEM((NY, 8, n_part), F32),
        pltpu.VMEM((NZ, 8, n_part), F32),
        pltpu.VMEM((NX, 8, n_part), F32),
        dma((8,)),
        dma((NZ,)), dma((NZ,)),
        dma((NY, NZ)), dma((NY, NZ)),
        dma((NY,)), dma((NY,)),
        dma((NX,)), dma((NX,)),
        dma((4,)), dma((4,)),
        dma((4,)), dma((4,)),
        dma((NZ,)), dma((NZ,)),
        dma((NX,)), dma((NX,)),
        dma, dma,
        dma((NY,)), dma((NY,)),
        dma((NZ,)), dma((NZ,)),
        dma((NX,)), dma((NX,)),
    ]
    moved, le, ess = pl.pallas_call(
        kernel,
        out_shape=(
            jax.ShapeDtypeStruct((cols, n_part), F32),
            jax.ShapeDtypeStruct((1, 1), F32),
            jax.ShapeDtypeStruct((1, 1), F32),
        ),
        in_specs=[pl.BlockSpec(memory_space=pl.ANY), vmem, vmem, smem, vmem, vmem, vmem, vmem, smem, smem, smem],
        out_specs=(vmem, vmem, vmem),
        scratch_shapes=scratch,
        compiler_params=pltpu.CompilerParams(collective_id=0, has_side_effects=True, vmem_limit_bytes=56 << 20),
        cost_estimate=pl.CostEstimate(flops=4 * n_rec * n_feat * n_part, bytes_accessed=2 * n_rec * n_feat, transcendentals=n_rec * n_part),
    )(
        records, counts_obs.reshape(-1, 128), exposure_bin.reshape(-1, 128), bin_offset, theta.T, noise.T,
        offspring.reshape(-1, 128), slot_order.reshape(-1, 128),
        temper_step.reshape(1), temper_level.reshape(1), step_size.reshape(1),
    )
    return moved.T, le[0, 0], ess[0, 0]


def solution(mesh):
    in_specs = (P("dp", None), P("dp"), P("dp"), P(), P("dom", "dp"), P("dom", "dp"), P(), P(), P(), P(), P())
    out_specs = (P("dom", "dp"), P(), P())
    return jax.shard_map(on_device, mesh=mesh, in_specs=in_specs, out_specs=out_specs, check_vma=False)
```

```python
import math

import jax
import jax.numpy as jnp
from jax import lax
from jax.experimental import pallas as pl
from jax.experimental.pallas import tpu as pltpu
from jax.sharding import PartitionSpec as P

F32, BF16 = jnp.float32, jnp.bfloat16
MESH = pl.DeviceIdType.MESH
NZ, NY, NX, NH = 8, 4, 4, 2
NEAR = (1, 7)
FAR = (2, 6, 3, 5, 4)
SCORE_STEPS = ((4, 3), (5, 2), (6, 1), (7, 0))


def kernel(
    rec_hbm, cnt_hbm, bin_hbm, bo_hbm, th_hbm, nz_hbm, offs_hbm, slot_hbm, tstep_hbm, tlev_hbm, step_hbm,
    out_ref, le_ref, ess_ref,
    rec, rect, thg, res, offb, cntb, sel, thx, acc, scf, snd_c, rcv_c, snd_n, rcv_n, snd_y, rcv_y, snd_z, rcv_z, scx,
    ll_own, ll_c, ll_y, ll_z, ll_x, cnt_v, bin_v, th_v, nz_v, offs_v, slot_v, bo_s, tstep_s, tlev_s, step_s,
    rec_sem, in_sem, sent, gz_r, gy_r, gc_r, tx_r, c_r, n_r, y_r, z_r, x_r, lc_r, ly_r, lz_r, lx_r,
):
    x = lax.axis_index("dom")
    dp = lax.axis_index("dp")
    z, y, c = dp // 8, (dp // 2) % 4, dp % 2
    n_rec, n_feat = rec.shape
    n_part = th_v.shape[1]
    half = n_part // NH
    scale_in = 1.0 / math.sqrt(n_feat)
    temper_scale = math.sqrt(n_feat / (n_rec * NZ * NY * 2))

    def at(zz, yy, cc):
        return (x, zz * 8 + yy * 2 + cc)

    sib = at(z, y, 1 - c)
    zs = [lax.rem(z + k, NZ) for k in range(NZ)]
    ys = [lax.rem(y + k, NY) for k in range(NY)]
    xs = [lax.rem(x + k, NX) for k in range(NX)]
    z_from = [lax.rem(z + NZ - k, NZ) for k in range(NZ)]
    y_from = [lax.rem(y + NY - k, NY) for k in range(NY)]
    x_from = [lax.rem(x + NX - k, NX) for k in range(NX)]

    barrier = pltpu.get_barrier_semaphore()
    peers = [at(zs[k], y, c) for k in FAR[::-1] + NEAR] + [at(z, ys[k], c) for k in (2, 1, 3)] + [(xs[k], dp) for k in (2, 1, 3)] + [sib]
    for peer in peers:
        pl.semaphore_signal(barrier, inc=1, device_id=peer, device_id_type=MESH)

    def load(src, dst, sem):
        cp = pltpu.make_async_copy(src, dst, sem)
        cp.start()
        return cp

    th_in = load(th_hbm, th_v, in_sem.at[0])
    small = [
        load(s, d, in_sem.at[1 + i])
        for i, (s, d) in enumerate(
            ((bo_hbm, bo_s), (bin_hbm, bin_v), (cnt_hbm, cnt_v), (nz_hbm, nz_v), (offs_hbm, offs_v), (slot_hbm, slot_v),
             (tstep_hbm, tstep_s), (tlev_hbm, tlev_s), (step_hbm, step_s))
        )
    ]
    blk = n_rec // 4
    loads = [load(rec_hbm.at[pl.ds(i * blk, blk)], rec.at[pl.ds(i * blk, blk)], rec_sem.at[i]) for i in range(4)]

    th_in.wait()
    theta = th_v[...]
    for h in range(NH):
        thg[h, z, y, c] = theta[:, h * half : (h + 1) * half].astype(BF16)
    thx[x] = theta
    for cp in small:
        cp.wait()

    pl.semaphore_wait(barrier, len(peers))

    sends = []

    def send(src, dst, rs, dev):
        cp = pltpu.make_async_remote_copy(src_ref=src, dst_ref=dst, send_sem=sent, recv_sem=rs, device_id=dev, device_id_type=MESH)
        cp.start()
        sends.append(math.prod(src.shape) * src.dtype.itemsize)

    def arrived(dst, rs):
        pltpu.make_async_remote_copy(src_ref=dst, dst_ref=dst, send_sem=rs, recv_sem=rs, device_id=sib, device_id_type=MESH).wait_recv()

    def to_y(h, k):
        part = thg.at[h, z_from[k], y, c]
        for j in (2, 1, 3):
            send(part, part, gy_r.at[h, k], at(z, ys[j], c))

    def to_near(h):
        arrived(thg.at[h, z, pl.ds(0, 3), c], gy_r.at[h, 0])
        for j in (1, 3, 2):
            part = thg.at[h, z, y_from[j], c]
            for k in NEAR:
                send(part, part, gz_r.at[h, k], at(zs[k], y, c))

    def to_sib(h, k):
        if k in NEAR:
            arrived(thg.at[h, z_from[k], :, c], gz_r.at[h, k])
        elif k in FAR:
            arrived(thg.at[h, z_from[k], pl.ds(0, 3), c], gy_r.at[h, k])
        part = thg.at[h, z_from[k], :, c]
        send(part, part, gc_r.at[h], sib)

    def gathered(h):
        arrived(thg.at[h, :, :, c], gc_r.at[h])

    for h in range(NH):
        part = thg.at[h, z, y, c]
        for k in FAR + NEAR:
            send(part, part, gz_r.at[h, k], at(zs[k], y, c))
        to_y(h, 0)
    for k in (2, 1, 3):
        send(thx.at[x], thx.at[x], tx_r, (xs[k], dp))

    bins = bin_v[...]
    off = jnp.zeros(bins.shape, F32)
    for b in range(bo_s.shape[0]):
        off = jnp.where(bins == b, bo_s[b], off)
    counts = cnt_v[...]
    table = jnp.zeros(counts.shape, F32)
    for n in range(2, 8):
        table = jnp.where(counts == n, math.lgamma(n + 1.0), table)
    log_factorial = jnp.sum(table)
    cntf = counts.astype(F32)
    for i in range(n_rec // 128):
        rows = pl.ds(128 * i, 128)
        offb[rows, :] = jnp.broadcast_to(off[i : i + 1, :], (128, 128)).T
        cntb[rows, :] = jnp.broadcast_to(cntf[i : i + 1, :], (128, 128)).T

    def transpose_block(i):
        loads[i].wait()
        rect[:, :, :, pl.ds(i * blk, blk)] = rec[pl.ds(i * blk, blk), :].T.reshape(NZ, NY, 64, blk)

    for i in range(2):
        transpose_block(i)
    to_near(0)
    to_near(1)
    for h in range(NH):
        for k in FAR:
            arrived(thg.at[h, z_from[k], y, c], gz_r.at[h, k])
            to_y(h, k)
        to_sib(h, 0)
    for i in range(2, 4):
        transpose_block(i)

    ll_own[...] = jnp.full(ll_own.shape, -log_factorial / 8.0, F32)

    def matmul1(h, i):
        rows = pl.ds(i * 512, 512)
        prod = jnp.dot(rec[rows, :], thg[h].reshape(n_feat, half), preferred_element_type=F32)
        o, t = offb[rows, :], cntb[rows, :]
        for q in range(half // 128):
            lanes = slice(128 * q, 128 * q + 128)
            out_lanes = slice(h * half + 128 * q, h * half + 128 * q + 128)
            lin = prod[:, lanes] * scale_in + o
            inten = jnp.exp(lin)
            ll_own[:, out_lanes] += jnp.sum((t * lin - inten).reshape(64, 8, 128), axis=0)
            res[h, rows, lanes] = (t - inten).astype(BF16)

    def matmul2(h, s):
        for i, k in enumerate(SCORE_STEPS[s]):
            part = jnp.dot(rect[zs[k]].reshape(256, n_rec), res[h], preferred_element_type=F32)
            scf[h, k] = part.reshape(NY, 2, 32, half)
            snd_c[h, s, i] = scf[h, k, :, 1 - c].astype(BF16)
        send(snd_c.at[h, s], rcv_c.at[h, s], c_r.at[h, s], sib)

    def y_send(h, k):
        for j in (2, 1, 3):
            send(snd_y.at[h, k, ys[j]], rcv_y.at[h, k, j], y_r.at[h, k], at(z, ys[j], c))

    def chip_sum(h, s):
        arrived(rcv_c.at[h, s], c_r.at[h, s])
        for i, k in enumerate(SCORE_STEPS[s]):
            total = scf[h, k, :, c] + rcv_c[h, s, i].astype(F32)
            if k in NEAR:
                snd_n[h, k // 7] = total.astype(BF16)
                send(snd_n.at[h, k // 7], rcv_n.at[h, k // 7], n_r.at[h], at(zs[k], y, c))
            else:
                scf[h, k, :, 0] = total
                if k:
                    snd_y[h, k] = total.astype(BF16)
                    y_send(h, k)

    def near_sum(h):
        total = scf[h, 0, :, 0]
        arrived(rcv_n.at[h], n_r.at[h])
        for i in range(2):
            total = total + rcv_n[h, i].astype(F32)
        scf[h, 0, :, 0] = total
        snd_y[h, 0] = total.astype(BF16)
        y_send(h, 0)

    def y_sum(h, k):
        total = scf[h, k, y, 0]
        arrived(rcv_y.at[h, k, pl.ds(0, 3)], y_r.at[h, k])
        for j in (1, 3, 2):
            total = total + rcv_y[h, k, j].astype(F32)
        return total

    def far_send(h, k):
        snd_z[h, k] = y_sum(h, k).astype(BF16)
        send(snd_z.at[h, k], rcv_z.at[h, k], z_r.at[h], at(zs[k], y, c))

    def z_sum(h):
        score = y_sum(h, 0)
        arrived(rcv_z.at[h, pl.ds(0, 5)], z_r.at[h])
        for k in FAR:
            score = score + rcv_z[h, k].astype(F32)
        scx[h, x] = score.astype(BF16)
        for k in (2, 1, 3):
            send(scx.at[h, x], scx.at[h, x], x_r.at[h], (xs[k], dp))

    def resampled_score(h):
        arrived(scx.at[h, pl.ds(0, 3)], x_r.at[h])
        scores = jnp.concatenate([scx[h, q] for q in range(NX)], axis=1)
        return jnp.dot(scores, sel[:, h].reshape(NX * half, n_part), preferred_element_type=F32)

    for k in FAR + NEAR:
        to_sib(0, k)
    gathered(0)
    for i in range(4):
        matmul1(0, i)
    for k in (2, 6):
        to_sib(1, k)
    for i in range(4):
        matmul2(0, i)
        if i:
            chip_sum(0, i - 1)
    chip_sum(0, 3)
    for k in (3, 5, 4) + NEAR:
        to_sib(1, k)
    gathered(1)
    for i in range(4):
        matmul1(1, i)
    send(ll_own, ll_c, lc_r, sib)
    for i in range(4):
        matmul2(1, i)
        if i:
            chip_sum(1, i - 1)
        else:
            arrived(ll_c, lc_r)
            ll_y[y] = ll_own[...] + ll_c[...]
            for k in (2, 1, 3):
                send(ll_y.at[y], ll_y.at[y], ly_r, at(z, ys[k], c))
        if i == 2:
            near_sum(0)
    chip_sum(1, 3)
    for k in (4, 3, 5, 2, 6):
        far_send(0, k)
    near_sum(1)
    arrived(ll_y.at[pl.ds(0, 3)], ly_r)
    ll_z[z] = (ll_y[0] + ll_y[1]) + (ll_y[2] + ll_y[3])
    for k in FAR + NEAR:
        send(ll_z.at[z], ll_z.at[z], lz_r, at(zs[k], y, c))

    offs = offs_v[...].astype(F32)
    upper = (lax.broadcasted_iota(jnp.int32, (128, 128), 0) <= lax.broadcasted_iota(jnp.int32, (128, 128), 1)).astype(F32).astype(BF16)
    within = jnp.dot(offs.astype(BF16), upper, preferred_element_type=F32)
    slots = jnp.concatenate([slot_v[pl.ds(x * 4 + q, 1), :] for q in range(4)], axis=1).astype(F32)
    before = jnp.zeros((1, 1), F32)
    for i in range(offs.shape[0]):
        upto = within[i : i + 1, :] + before
        start = upto - offs[i : i + 1, :]
        upto_b = jnp.broadcast_to(upto, (128, 128)).T
        start_b = jnp.broadcast_to(start, (128, 128)).T
        for q in range(4):
            lanes = slice(128 * q, 128 * q + 128)
            hit = (slots[:, lanes] >= start_b) & (slots[:, lanes] < upto_b)
            sel[i // 4, (i % 4) // 2, 128 * (i % 2) : 128 * (i % 2) + 128, lanes] = jnp.where(hit, 1.0, 0.0).astype(BF16)
        before = before + within[i : i + 1, 127:128]

    arrived(thx.at[pl.ds(0, 3)], tx_r)
    everyone = jnp.concatenate([thx[q] for q in range(NX)], axis=1)
    hi = everyone.astype(BF16)
    rest = everyone - hi.astype(F32)
    mid = rest.astype(BF16)
    lo = (rest - mid.astype(F32)).astype(BF16)
    taken = jnp.dot(jnp.concatenate([hi, mid, lo], axis=0), sel[...].reshape(NX * n_part, n_part), preferred_element_type=F32)
    taken = taken[0:32] + taken[32:64] + taken[64:96]
    step = step_s[0]
    root = jnp.sqrt(jnp.full((1, 1), step, F32))
    acc[...] = (1.0 - 0.5 * step) * taken + root * nz_v[...]
    gain = 0.5 * step * tlev_s[0] * (temper_scale * scale_in)

    for k in (4, 3, 5, 2, 6):
        far_send(1, k)
    z_sum(0)
    arrived(ll_z.at[pl.ds(0, 7)], lz_r)
    ll_x[x] = ((ll_z[0] + ll_z[1]) + (ll_z[2] + ll_z[3])) + ((ll_z[4] + ll_z[5]) + (ll_z[6] + ll_z[7]))
    for k in (2, 1, 3):
        send(ll_x.at[x], ll_x.at[x], lx_r, (xs[k], dp))
    acc[...] += gain * resampled_score(0)
    z_sum(1)

    arrived(ll_x.at[pl.ds(0, 3)], lx_r)
    loglik = jnp.concatenate([jnp.sum(ll_x[q], axis=0, keepdims=True) for q in range(NX)], axis=0)
    log_weight = tstep_s[0] * temper_scale * loglik
    peak = jnp.max(log_weight, axis=(0, 1), keepdims=True)
    shifted = jnp.exp(log_weight - peak)
    weight_sum = jnp.sum(shifted, axis=(0, 1), keepdims=True)
    weight_square = jnp.sum(shifted * shifted, axis=(0, 1), keepdims=True)
    le_ref[...] = peak + jnp.log(weight_sum) - math.log(NX * n_part)
    ess_ref[...] = weight_sum * weight_sum / (weight_square * (NX * n_part))

    out_ref[...] = acc[...] + gain * resampled_score(1)

    everything = rec.at[pl.ds(0, sum(sends) // (2 * n_feat))]
    pltpu.make_async_remote_copy(src_ref=everything, dst_ref=everything, send_sem=sent, recv_sem=sent, device_id=sib, device_id_type=MESH).wait_send()


def hand_over(*refs):
    for i in range(3):
        refs[3 + i][...] = refs[i][...]


def on_device(records, counts_obs, exposure_bin, bin_offset, theta, noise, offspring, slot_order, temper_step, temper_level, step_size):
    n_rec, n_feat = records.shape
    n_part, cols = theta.shape
    half = n_part // NH
    vmem, anywhere = pl.BlockSpec(memory_space=pltpu.VMEM), pl.BlockSpec(memory_space=pl.ANY)
    dma = pltpu.SemaphoreType.DMA
    counts_obs, exposure_bin, offspring, slot_order = (a.reshape(-1, 128) for a in (counts_obs, exposure_bin, offspring, slot_order))
    scratch = [
        pltpu.VMEM((n_rec, n_feat), BF16),
        pltpu.VMEM((NZ, NY, 64, n_rec), BF16),
        pltpu.VMEM((NH, NZ, NY, 2, cols, half), BF16),
        pltpu.VMEM((NH, n_rec, half), BF16),
        pltpu.VMEM((n_rec, 128), F32),
        pltpu.VMEM((n_rec, 128), F32),
        pltpu.VMEM((NX, NH, half, n_part), BF16),
        pltpu.VMEM((NX, cols, n_part), F32),
        pltpu.VMEM((cols, n_part), F32),
        pltpu.VMEM((NH, NZ, NY, 2, cols, half), F32),
        pltpu.VMEM((NH, 4, 2, NY, cols, half), BF16),
        pltpu.VMEM((NH, 4, 2, NY, cols, half), BF16),
        pltpu.VMEM((NH, 2, NY, cols, half), BF16),
        pltpu.VMEM((NH, 2, NY, cols, half), BF16),
        pltpu.VMEM((NH, NZ, NY, cols, half), BF16),
        pltpu.VMEM((NH, NZ, NY, cols, half), BF16),
        pltpu.VMEM((NH, NZ, cols, half), BF16),
        pltpu.VMEM((NH, NZ, cols, half), BF16),
        pltpu.VMEM((NH, NX, cols, half), BF16),
        pltpu.VMEM((8, n_part), F32),
        pltpu.VMEM((8, n_part), F32),
        pltpu.VMEM((NY, 8, n_part), F32),
        pltpu.VMEM((NZ, 8, n_part), F32),
        pltpu.VMEM((NX, 8, n_part), F32),
        pltpu.VMEM(counts_obs.shape, jnp.int32),
        pltpu.VMEM(exposure_bin.shape, jnp.int32),
        pltpu.VMEM((cols, n_part), F32),
        pltpu.VMEM((cols, n_part), F32),
        pltpu.VMEM(offspring.shape, jnp.int32),
        pltpu.VMEM(slot_order.shape, jnp.int32),
        pltpu.SMEM(bin_offset.shape, F32),
        pltpu.SMEM((1,), F32), pltpu.SMEM((1,), F32), pltpu.SMEM((1,), F32),
        dma((4,)), dma((10,)), dma,
        dma((NH, NZ)), dma((NH, NZ)), dma((NH,)), dma,
        dma((NH, 4)), dma((NH,)), dma((NH, NZ)), dma((NH,)), dma((NH,)),
        dma, dma, dma, dma,
    ]
    shapes = (
        jax.ShapeDtypeStruct((cols, n_part), F32),
        jax.ShapeDtypeStruct((1, 1), F32),
        jax.ShapeDtypeStruct((1, 1), F32),
    )
    results = pl.pallas_call(
        kernel,
        out_shape=shapes,
        in_specs=[anywhere] * 11,
        out_specs=(vmem, vmem, vmem),
        scratch_shapes=scratch,
        compiler_params=pltpu.CompilerParams(collective_id=0, has_side_effects=True, vmem_limit_bytes=60 << 20),
        cost_estimate=pl.CostEstimate(flops=4 * n_rec * n_feat * n_part, bytes_accessed=2 * n_rec * n_feat, transcendentals=n_rec * n_part),
    )(
        records, counts_obs, exposure_bin, bin_offset, theta.T, noise.T, offspring, slot_order,
        temper_step.reshape(1), temper_level.reshape(1), step_size.reshape(1),
    )
    moved, le, ess = pl.pallas_call(
        hand_over,
        out_shape=shapes,
        in_specs=[vmem] * 3,
        out_specs=(vmem,) * 3,
    )(*results)
    return moved.T, le[0, 0], ess[0, 0]


def solution(mesh):
    in_specs = (P("dp", None), P("dp"), P("dp"), P(), P("dom", "dp"), P("dom", "dp"), P(), P(), P(), P(), P())
    out_specs = (P("dom", "dp"), P(), P())
    return jax.shard_map(on_device, mesh=mesh, in_specs=in_specs, out_specs=out_specs, check_vma=False)
```

```python
import math

import jax
import jax.numpy as jnp
from jax import lax
from jax.experimental import pallas as pl
from jax.experimental.pallas import tpu as pltpu
from jax.sharding import PartitionSpec as P

F32, BF16 = jnp.float32, jnp.bfloat16
MESH = pl.DeviceIdType.MESH
NZ, NY, NX, NH = 8, 4, 4, 2
NEAR = (1, 7)
FAR = (2, 6, 4, 3, 5)
SCORE_STEPS = ((4, 3), (1, 7), (5, 2), (6, 0))


def kernel(
    rec_hbm, cnt_hbm, bin_hbm, bo_hbm, th_hbm, nz_hbm, offs_hbm, slot_hbm, tstep_hbm, tlev_hbm, step_hbm,
    out_ref, le_ref, ess_ref,
    rec, rect, thg, res, offb, cntb, sel, thx, acc, scf, snd_c, rcv_c, snd_n, rcv_n, snd_y, rcv_y, snd_z, rcv_z, scx,
    ll_own, ll_rows, cnt_v, bin_v, th_v, nz_v, offs_v, slot_v, bo_s, tstep_s, tlev_s, step_s,
    rec_sem, in_sem, sent, row_sent, x_sent, gz_r, gy_r, gc_r, tx_r, c_r, n_r, y_r, z_r, x_r, lc_r, ly_r, lz_r, lx_r,
):
    x = lax.axis_index("dom")
    dp = lax.axis_index("dp")
    z, y, c = dp // 8, (dp // 2) % 4, dp % 2
    n_rec, n_feat = rec.shape
    n_part = th_v.shape[1]
    half = n_part // NH
    scale_in = 1.0 / math.sqrt(n_feat)
    temper_scale = math.sqrt(n_feat / (n_rec * NZ * NY * 2))

    def at(zz, yy, cc):
        return (x, zz * 8 + yy * 2 + cc)

    sib = at(z, y, 1 - c)
    zs = [lax.rem(z + k, NZ) for k in range(NZ)]
    ys = [lax.rem(y + k, NY) for k in range(NY)]
    xs = [lax.rem(x + k, NX) for k in range(NX)]
    z_from = [lax.rem(z + NZ - k, NZ) for k in range(NZ)]
    y_from = [lax.rem(y + NY - k, NY) for k in range(NY)]
    x_from = [lax.rem(x + NX - k, NX) for k in range(NX)]

    barrier = pltpu.get_barrier_semaphore()
    peers = [at(zs[k], y, c) for k in FAR[::-1] + NEAR] + [at(z, ys[k], c) for k in (2, 1, 3)] + [(xs[k], dp) for k in (2, 1, 3)] + [sib]
    for peer in peers:
        pl.semaphore_signal(barrier, inc=1, device_id=peer, device_id_type=MESH)

    def load(src, dst, sem):
        cp = pltpu.make_async_copy(src, dst, sem)
        cp.start()
        return cp

    th_in = load(th_hbm, th_v, in_sem.at[0])
    small = [
        load(s, d, in_sem.at[1 + i])
        for i, (s, d) in enumerate(
            ((bo_hbm, bo_s), (bin_hbm, bin_v), (cnt_hbm, cnt_v), (nz_hbm, nz_v), (offs_hbm, offs_v), (slot_hbm, slot_v),
             (tstep_hbm, tstep_s), (tlev_hbm, tlev_s), (step_hbm, step_s))
        )
    ]
    blk = n_rec // 4
    loads = [load(rec_hbm.at[pl.ds(i * blk, blk)], rec.at[pl.ds(i * blk, blk)], rec_sem.at[i]) for i in range(4)]

    th_in.wait()
    theta = th_v[...]
    for h in range(NH):
        thg[h, z, y, c] = theta[:, h * half : (h + 1) * half].astype(BF16)
    thx[x] = theta
    for cp in small:
        cp.wait()

    pl.semaphore_wait(barrier, len(peers))

    sends = []

    def send(src, dst, rs, dev, ss=None):
        row = src.shape[-2] == 1
        cp = pltpu.make_async_remote_copy(
            src_ref=src, dst_ref=dst, send_sem=ss if ss is not None else row_sent if row else sent, recv_sem=rs, device_id=dev, device_id_type=MESH
        )
        cp.start()
        if not row and ss is None:
            sends.append(math.prod(src.shape) * src.dtype.itemsize)

    def arrived(dst, rs):
        pltpu.make_async_remote_copy(src_ref=dst, dst_ref=dst, send_sem=rs, recv_sem=rs, device_id=sib, device_id_type=MESH).wait_recv()

    def to_y(h, k):
        part = thg.at[h, z_from[k], y, c]
        for j in (2, 1, 3):
            send(part, part, gy_r.at[h, k], at(z, ys[j], c))

    def to_near(h):
        arrived(thg.at[h, z, pl.ds(0, 3), c], gy_r.at[h, 0])
        for j in (1, 3, 2):
            part = thg.at[h, z, y_from[j], c]
            for k in NEAR:
                send(part, part, gz_r.at[h, k], at(zs[k], y, c))

    def to_sib(h, k):
        if k in NEAR:
            arrived(thg.at[h, z_from[k], :, c], gz_r.at[h, k])
        elif k in FAR:
            arrived(thg.at[h, z_from[k], pl.ds(0, 3), c], gy_r.at[h, k])
        part = thg.at[h, z_from[k], :, c]
        send(part, part, gc_r.at[h], sib)

    def gathered(h):
        arrived(thg.at[h, :, :, c], gc_r.at[h])

    for h in range(NH):
        part = thg.at[h, z, y, c]
        for k in FAR + NEAR:
            send(part, part, gz_r.at[h, k], at(zs[k], y, c))
        to_y(h, 0)
    for k in (2, 1, 3):
        send(thx.at[x], thx.at[x], tx_r, (xs[k], dp))

    bins = bin_v[...]
    off = jnp.zeros(bins.shape, F32)
    for b in range(bo_s.shape[0]):
        off = jnp.where(bins == b, bo_s[b], off)
    counts = cnt_v[...]
    table = jnp.zeros(counts.shape, F32)
    for n in range(2, 8):
        table = jnp.where(counts == n, math.lgamma(n + 1.0), table)
    log_factorial = jnp.sum(table)
    cntf = counts.astype(F32)
    for i in range(n_rec // 128):
        rows = pl.ds(128 * i, 128)
        offb[rows, :] = jnp.broadcast_to(off[i : i + 1, :], (128, 128)).T
        cntb[rows, :] = jnp.broadcast_to(cntf[i : i + 1, :], (128, 128)).T

    def transpose_block(i):
        loads[i].wait()
        rect[:, :, :, pl.ds(i * blk, blk)] = rec[pl.ds(i * blk, blk), :].T.reshape(NZ, NY, 64, blk)

    for i in range(2):
        transpose_block(i)
    to_near(0)
    to_near(1)
    for h in range(NH):
        for i, k in enumerate(FAR):
            arrived(thg.at[h, z_from[k], y, c], gz_r.at[h, k])
            to_y(h, k)
            if h == 0 and i in (1, 3):
                transpose_block(2 + i // 2)
            if h == 1:
                to_sib(0, k)
        if h == 0:
            to_sib(0, 0)

    ll_own[...] = jnp.full(ll_own.shape, -log_factorial / 8.0, F32)

    def matmul1(h, i):
        rows = pl.ds(i * 512, 512)
        prod = jnp.dot(rec[rows, :], thg[h].reshape(n_feat, half), preferred_element_type=F32)
        o, t = offb[rows, :], cntb[rows, :]
        for q in range(half // 128):
            lanes = slice(128 * q, 128 * q + 128)
            out_lanes = slice(h * half + 128 * q, h * half + 128 * q + 128)
            lin = prod[:, lanes] * scale_in + o
            inten = jnp.exp(lin)
            ll_own[:, out_lanes] += jnp.sum((t * lin - inten).reshape(64, 8, 128), axis=0)
            res[h, rows, lanes] = (t - inten).astype(BF16)

    def matmul2(h, s):
        for i, k in enumerate(SCORE_STEPS[s]):
            part = jnp.dot(rect[zs[k]].reshape(256, n_rec), res[h], preferred_element_type=F32)
            scf[h, k] = part.reshape(NY, 2, 32, half)
            snd_c[h, s, i] = scf[h, k, :, 1 - c].astype(BF16)
        send(snd_c.at[h, s], rcv_c.at[h, s], c_r.at[h, s], sib)

    def y_send(h, k):
        for j in (2, 1, 3):
            send(snd_y.at[h, k, ys[j]], rcv_y.at[h, k, j], y_r.at[h, k], at(z, ys[j], c))

    def chip_sum(h, s):
        arrived(rcv_c.at[h, s], c_r.at[h, s])
        for i, k in enumerate(SCORE_STEPS[s]):
            total = scf[h, k, :, c] + rcv_c[h, s, i].astype(F32)
            if k in NEAR:
                snd_n[h, k // 7] = total.astype(BF16)
                send(snd_n.at[h, k // 7], rcv_n.at[h, k // 7], n_r.at[h], at(zs[k], y, c))
            else:
                scf[h, k, :, 0] = total
                if k:
                    snd_y[h, k] = total.astype(BF16)
                    y_send(h, k)

    def near_sum(h):
        total = scf[h, 0, :, 0]
        arrived(rcv_n.at[h], n_r.at[h])
        for i in range(2):
            total = total + rcv_n[h, i].astype(F32)
        scf[h, 0, :, 0] = total
        snd_y[h, 0] = total.astype(BF16)
        y_send(h, 0)

    def y_sum(h, k):
        total = scf[h, k, y, 0]
        arrived(rcv_y.at[h, k, pl.ds(0, 3)], y_r.at[h, k])
        for j in (1, 3, 2):
            total = total + rcv_y[h, k, j].astype(F32)
        return total

    def far_send(h, k):
        snd_z[h, k] = y_sum(h, k).astype(BF16)
        send(snd_z.at[h, k], rcv_z.at[h, k], z_r.at[h], at(zs[k], y, c))

    def z_sum(h):
        score = y_sum(h, 0)
        arrived(rcv_z.at[h, pl.ds(0, 5)], z_r.at[h])
        for k in FAR:
            score = score + rcv_z[h, k].astype(F32)
        scx[h, x] = score.astype(BF16)
        for k in (2, 1, 3):
            send(scx.at[h, x], scx.at[h, x], x_r.at[h], (xs[k], dp), x_sent)

    def resampled_score(h):
        arrived(scx.at[h, pl.ds(0, 3)], x_r.at[h])
        scores = jnp.concatenate([scx[h, q] for q in range(NX)], axis=1)
        return jnp.dot(scores, sel[:, h].reshape(NX * half, n_part), preferred_element_type=F32)

    for k in NEAR:
        to_sib(0, k)
    to_sib(1, 0)
    gathered(0)
    for i in range(4):
        matmul1(0, i)
    for k in FAR + NEAR:
        to_sib(1, k)
    for i in range(4):
        matmul2(0, i)
        if i:
            chip_sum(0, i - 1)
    chip_sum(0, 3)
    gathered(1)
    for i in range(4):
        matmul1(1, i)
    ll_rows[0] = jnp.sum(ll_own[...], axis=0, keepdims=True)
    send(ll_rows.at[0], ll_rows.at[1], lc_r, sib)
    for i in range(4):
        matmul2(1, i)
        if i:
            chip_sum(1, i - 1)
        else:
            arrived(ll_rows.at[1], lc_r)
            ll_rows[2 + y] = ll_rows[0] + ll_rows[1]
            for k in (2, 1, 3):
                send(ll_rows.at[2 + y], ll_rows.at[2 + y], ly_r, at(z, ys[k], c))
    chip_sum(1, 3)
    arrived(ll_rows.at[pl.ds(2, 3)], ly_r)
    ll_rows[6 + z] = (ll_rows[2] + ll_rows[3]) + (ll_rows[4] + ll_rows[5])
    for k in FAR + NEAR:
        send(ll_rows.at[6 + z], ll_rows.at[6 + z], lz_r, at(zs[k], y, c))
    near_sum(0)
    for k in (4, 3, 5, 2, 6):
        far_send(0, k)
    offs = offs_v[...].astype(F32)
    upper = (lax.broadcasted_iota(jnp.int32, (128, 128), 0) <= lax.broadcasted_iota(jnp.int32, (128, 128), 1)).astype(F32).astype(BF16)
    within = jnp.dot(offs.astype(BF16), upper, preferred_element_type=F32)
    slots = jnp.concatenate([slot_v[pl.ds(x * 4 + q, 1), :] for q in range(4)], axis=1).astype(F32)
    before = jnp.zeros((1, 1), F32)
    for i in range(offs.shape[0]):
        upto = within[i : i + 1, :] + before
        start = upto - offs[i : i + 1, :]
        upto_b = jnp.broadcast_to(upto, (128, 128)).T
        start_b = jnp.broadcast_to(start, (128, 128)).T
        for q in range(4):
            lanes = slice(128 * q, 128 * q + 128)
            hit = (slots[:, lanes] >= start_b) & (slots[:, lanes] < upto_b)
            sel[i // 4, (i % 4) // 2, 128 * (i % 2) : 128 * (i % 2) + 128, lanes] = jnp.where(hit, 1.0, 0.0).astype(BF16)
        before = before + within[i : i + 1, 127:128]

    arrived(thx.at[pl.ds(0, 3)], tx_r)
    everyone = jnp.concatenate([thx[q] for q in range(NX)], axis=1)
    hi = everyone.astype(BF16)
    rest = everyone - hi.astype(F32)
    mid = rest.astype(BF16)
    lo = (rest - mid.astype(F32)).astype(BF16)
    taken = jnp.dot(jnp.concatenate([hi, mid, lo], axis=0), sel[...].reshape(NX * n_part, n_part), preferred_element_type=F32)
    taken = taken[0:32] + taken[32:64] + taken[64:96]
    step = step_s[0]
    root = jnp.sqrt(jnp.full((1, 1), step, F32))
    acc[...] = (1.0 - 0.5 * step) * taken + root * nz_v[...]
    gain = 0.5 * step * tlev_s[0] * (temper_scale * scale_in)

    near_sum(1)
    for k in (4, 3, 5, 2, 6):
        far_send(1, k)
    arrived(ll_rows.at[pl.ds(6, 7)], lz_r)
    rows = [ll_rows[6 + q] for q in range(NZ)]
    ll_rows[14 + x] = ((rows[0] + rows[1]) + (rows[2] + rows[3])) + ((rows[4] + rows[5]) + (rows[6] + rows[7]))
    for k in (2, 1, 3):
        send(ll_rows.at[14 + x], ll_rows.at[14 + x], lx_r, (xs[k], dp))
    z_sum(0)
    acc[...] += gain * resampled_score(0)
    z_sum(1)

    arrived(ll_rows.at[pl.ds(14, 3)], lx_r)
    loglik = jnp.concatenate([ll_rows[14 + q] for q in range(NX)], axis=0)
    log_weight = tstep_s[0] * temper_scale * loglik
    peak = jnp.max(log_weight, axis=(0, 1), keepdims=True)
    shifted = jnp.exp(log_weight - peak)
    weight_sum = jnp.sum(shifted, axis=(0, 1), keepdims=True)
    weight_square = jnp.sum(shifted * shifted, axis=(0, 1), keepdims=True)
    le_ref[...] = peak + jnp.log(weight_sum) - math.log(NX * n_part)
    ess_ref[...] = weight_sum * weight_sum / (weight_square * (NX * n_part))

    out_ref[...] = acc[...] + gain * resampled_score(1)

    part = scx.at[:, pl.ds(0, 3)]
    pltpu.make_async_remote_copy(src_ref=part, dst_ref=part, send_sem=x_sent, recv_sem=x_sent, device_id=sib, device_id_type=MESH).wait_send()
    rows_sent = ll_rows.at[pl.ds(0, 14)]
    pltpu.make_async_remote_copy(src_ref=rows_sent, dst_ref=rows_sent, send_sem=row_sent, recv_sem=row_sent, device_id=sib, device_id_type=MESH).wait_send()
    assert sum(sends) % (32 * n_feat) == 0
    everything = rec.at[pl.ds(0, sum(sends) // (2 * n_feat))]
    pltpu.make_async_remote_copy(src_ref=everything, dst_ref=everything, send_sem=sent, recv_sem=sent, device_id=sib, device_id_type=MESH).wait_send()


def hand_over(*refs):
    for i in range(3):
        refs[3 + i][...] = refs[i][...]


def on_device(records, counts_obs, exposure_bin, bin_offset, theta, noise, offspring, slot_order, temper_step, temper_level, step_size):
    n_rec, n_feat = records.shape
    n_part, cols = theta.shape
    half = n_part // NH
    vmem, anywhere = pl.BlockSpec(memory_space=pltpu.VMEM), pl.BlockSpec(memory_space=pl.ANY)
    dma = pltpu.SemaphoreType.DMA
    counts_obs, exposure_bin, offspring, slot_order = (a.reshape(-1, 128) for a in (counts_obs, exposure_bin, offspring, slot_order))
    scratch = [
        pltpu.VMEM((n_rec, n_feat), BF16),
        pltpu.VMEM((NZ, NY, 64, n_rec), BF16),
        pltpu.VMEM((NH, NZ, NY, 2, cols, half), BF16),
        pltpu.VMEM((NH, n_rec, half), BF16),
        pltpu.VMEM((n_rec, 128), F32),
        pltpu.VMEM((n_rec, 128), F32),
        pltpu.VMEM((NX, NH, half, n_part), BF16),
        pltpu.VMEM((NX, cols, n_part), F32),
        pltpu.VMEM((cols, n_part), F32),
        pltpu.VMEM((NH, NZ, NY, 2, cols, half), F32),
        pltpu.VMEM((NH, 4, 2, NY, cols, half), BF16),
        pltpu.VMEM((NH, 4, 2, NY, cols, half), BF16),
        pltpu.VMEM((NH, 2, NY, cols, half), BF16),
        pltpu.VMEM((NH, 2, NY, cols, half), BF16),
        pltpu.VMEM((NH, NZ, NY, cols, half), BF16),
        pltpu.VMEM((NH, NZ, NY, cols, half), BF16),
        pltpu.VMEM((NH, NZ, cols, half), BF16),
        pltpu.VMEM((NH, NZ, cols, half), BF16),
        pltpu.VMEM((NH, NX, cols, half), BF16),
        pltpu.VMEM((8, n_part), F32),
        pltpu.VMEM((2 + NY + NZ + NX, 1, n_part), F32),
        pltpu.VMEM(counts_obs.shape, jnp.int32),
        pltpu.VMEM(exposure_bin.shape, jnp.int32),
        pltpu.VMEM((cols, n_part), F32),
        pltpu.VMEM((cols, n_part), F32),
        pltpu.VMEM(offspring.shape, jnp.int32),
        pltpu.VMEM(slot_order.shape, jnp.int32),
        pltpu.SMEM(bin_offset.shape, F32),
        pltpu.SMEM((1,), F32), pltpu.SMEM((1,), F32), pltpu.SMEM((1,), F32),
        dma((4,)), dma((10,)), dma, dma, dma,
        dma((NH, NZ)), dma((NH, NZ)), dma((NH,)), dma,
        dma((NH, 4)), dma((NH,)), dma((NH, NZ)), dma((NH,)), dma((NH,)),
        dma, dma, dma, dma,
    ]
    shapes = (
        jax.ShapeDtypeStruct((cols, n_part), F32),
        jax.ShapeDtypeStruct((1, 1), F32),
        jax.ShapeDtypeStruct((1, 1), F32),
    )
    results = pl.pallas_call(
        kernel,
        out_shape=shapes,
        in_specs=[anywhere] * 11,
        out_specs=(vmem, vmem, vmem),
        scratch_shapes=scratch,
        compiler_params=pltpu.CompilerParams(collective_id=0, has_side_effects=True, vmem_limit_bytes=60 << 20),
        cost_estimate=pl.CostEstimate(flops=4 * n_rec * n_feat * n_part, bytes_accessed=2 * n_rec * n_feat, transcendentals=n_rec * n_part),
    )(
        records, counts_obs, exposure_bin, bin_offset, theta.T, noise.T, offspring, slot_order,
        temper_step.reshape(1), temper_level.reshape(1), step_size.reshape(1),
    )
    moved, le, ess = pl.pallas_call(
        hand_over,
        out_shape=shapes,
        in_specs=[vmem] * 3,
        out_specs=(vmem,) * 3,
    )(*results)
    return moved.T, le[0, 0], ess[0, 0]


def solution(mesh):
    in_specs = (P("dp", None), P("dp"), P("dp"), P(), P("dom", "dp"), P("dom", "dp"), P(), P(), P(), P(), P())
    out_specs = (P("dom", "dp"), P(), P())
    return jax.shard_map(on_device, mesh=mesh, in_specs=in_specs, out_specs=out_specs, check_vma=False)
```

```python
import math

import jax
import jax.numpy as jnp
from jax import lax
from jax.experimental import pallas as pl
from jax.experimental.pallas import tpu as pltpu
from jax.sharding import PartitionSpec as P

F32, BF16 = jnp.float32, jnp.bfloat16
MESH = pl.DeviceIdType.MESH
NZ, NY, NX, NH = 8, 4, 4, 2
NEAR = (1, 7)
FAR = (2, 6, 4, 3, 5)
SCORE_STEPS = ((4, 3), (1, 7), (5, 2), (6, 0))


def kernel(
    rec_hbm, cnt_hbm, bin_hbm, bo_hbm, th_hbm, nz_hbm, offs_hbm, slot_hbm, tstep_hbm, tlev_hbm, step_hbm,
    out_ref, le_ref, ess_ref,
    rec, rect, thg, res, offb, cntb, sel, thx, acc, scf, snd_c, rcv_c, snd_n, rcv_n, snd_y, rcv_y, snd_z, rcv_z, scx,
    ll_own, ll_rows, cnt_v, bin_v, th_v, nz_v, offs_v, slot_v, bo_s, tstep_s, tlev_s, step_s,
    rec_sem, in_sem, sent, row_sent, x_sent, gz_r, gy_r, gc_r, tx_r, c_r, n_r, y_r, z_r, x_r, lc_r, ly_r, lz_r, lx_r,
):
    x = lax.axis_index("dom")
    dp = lax.axis_index("dp")
    z, y, c = dp // 8, (dp // 2) % 4, dp % 2
    n_rec, n_feat = rec.shape
    n_part = th_v.shape[1]
    half = n_part // NH
    scale_in = 1.0 / math.sqrt(n_feat)
    temper_scale = math.sqrt(n_feat / (n_rec * NZ * NY * 2))

    def at(zz, yy, cc):
        return (x, zz * 8 + yy * 2 + cc)

    sib = at(z, y, 1 - c)
    zs = [lax.rem(z + k, NZ) for k in range(NZ)]
    ys = [lax.rem(y + k, NY) for k in range(NY)]
    xs = [lax.rem(x + k, NX) for k in range(NX)]
    z_from = [lax.rem(z + NZ - k, NZ) for k in range(NZ)]
    y_from = [lax.rem(y + NY - k, NY) for k in range(NY)]
    x_from = [lax.rem(x + NX - k, NX) for k in range(NX)]

    barrier = pltpu.get_barrier_semaphore()
    peers = [at(zs[k], y, c) for k in FAR[::-1] + NEAR] + [at(z, ys[k], c) for k in (2, 1, 3)] + [(xs[k], dp) for k in (2, 1, 3)] + [sib]
    for peer in peers:
        pl.semaphore_signal(barrier, inc=1, device_id=peer, device_id_type=MESH)

    def load(src, dst, sem):
        cp = pltpu.make_async_copy(src, dst, sem)
        cp.start()
        return cp

    th_in = load(th_hbm, th_v, in_sem.at[0])
    small = [
        load(s, d, in_sem.at[1 + i])
        for i, (s, d) in enumerate(
            ((bo_hbm, bo_s), (bin_hbm, bin_v), (cnt_hbm, cnt_v), (nz_hbm, nz_v), (offs_hbm, offs_v), (slot_hbm, slot_v),
             (tstep_hbm, tstep_s), (tlev_hbm, tlev_s), (step_hbm, step_s))
        )
    ]
    blk = n_rec // 4
    loads = [load(rec_hbm.at[pl.ds(i * blk, blk)], rec.at[pl.ds(i * blk, blk)], rec_sem.at[i]) for i in range(4)]

    th_in.wait()
    theta = th_v[...]
    for h in range(NH):
        thg[h, z, y, c] = theta[:, h * half : (h + 1) * half].astype(BF16)
    thx[x] = theta
    for cp in small:
        cp.wait()

    pl.semaphore_wait(barrier, len(peers))

    sends = []

    def send(src, dst, rs, dev, ss=None):
        row = src.shape[-2] == 1
        cp = pltpu.make_async_remote_copy(
            src_ref=src, dst_ref=dst, send_sem=ss if ss is not None else row_sent if row else sent, recv_sem=rs, device_id=dev, device_id_type=MESH
        )
        cp.start()
        if not row and ss is None:
            sends.append(math.prod(src.shape) * src.dtype.itemsize)

    def arrived(dst, rs):
        pltpu.make_async_remote_copy(src_ref=dst, dst_ref=dst, send_sem=rs, recv_sem=rs, device_id=sib, device_id_type=MESH).wait_recv()

    def to_y(h, k):
        part = thg.at[h, z_from[k], y, c]
        for j in (2, 1, 3):
            send(part, part, gy_r.at[h, k], at(z, ys[j], c))

    def to_near(h):
        arrived(thg.at[h, z, pl.ds(0, 3), c], gy_r.at[h, 0])
        for j in (1, 3, 2):
            part = thg.at[h, z, y_from[j], c]
            for k in NEAR:
                send(part, part, gz_r.at[h, k], at(zs[k], y, c))

    def to_sib(h, k):
        if k in NEAR:
            arrived(thg.at[h, z_from[k], :, c], gz_r.at[h, k])
        elif k in FAR:
            arrived(thg.at[h, z_from[k], pl.ds(0, 3), c], gy_r.at[h, k])
        part = thg.at[h, z_from[k], :, c]
        send(part, part, gc_r.at[h], sib)

    def gathered(h):
        arrived(thg.at[h, :, :, c], gc_r.at[h])

    for ks in (FAR, NEAR):
        for h in range(NH):
            part = thg.at[h, z, y, c]
            for k in ks:
                send(part, part, gz_r.at[h, k], at(zs[k], y, c))
            if ks == FAR:
                to_y(h, 0)
    for k in (2, 1, 3):
        send(thx.at[x], thx.at[x], tx_r, (xs[k], dp))

    bins = bin_v[...]
    off = jnp.zeros(bins.shape, F32)
    for b in range(bo_s.shape[0]):
        off = jnp.where(bins == b, bo_s[b], off)
    counts = cnt_v[...]
    table = jnp.zeros(counts.shape, F32)
    for n in range(2, 8):
        table = jnp.where(counts == n, math.lgamma(n + 1.0), table)
    log_factorial = jnp.sum(table)
    cntf = counts.astype(F32)
    for i in range(n_rec // 128):
        rows = pl.ds(128 * i, 128)
        offb[rows, :] = jnp.broadcast_to(off[i : i + 1, :], (128, 128)).T
        cntb[rows, :] = jnp.broadcast_to(cntf[i : i + 1, :], (128, 128)).T

    def transpose_block(i):
        loads[i].wait()
        rect[:, :, :, pl.ds(i * blk, blk)] = rec[pl.ds(i * blk, blk), :].T.reshape(NZ, NY, 64, blk)

    for i in range(2):
        transpose_block(i)
    to_near(0)
    to_near(1)
    for h in range(NH):
        for i, k in enumerate(FAR):
            arrived(thg.at[h, z_from[k], y, c], gz_r.at[h, k])
            to_y(h, k)
            if h == 0 and i in (1, 3):
                transpose_block(2 + i // 2)
            if h == 1:
                to_sib(0, k)
        if h == 0:
            to_sib(0, 0)

    ll_own[...] = jnp.full(ll_own.shape, -log_factorial / 8.0, F32)

    def matmul1(h, i):
        rows = pl.ds(i * 512, 512)
        prod = jnp.dot(rec[rows, :], thg[h].reshape(n_feat, half), preferred_element_type=F32)
        o, t = offb[rows, :], cntb[rows, :]
        for q in range(half // 128):
            lanes = slice(128 * q, 128 * q + 128)
            out_lanes = slice(h * half + 128 * q, h * half + 128 * q + 128)
            lin = prod[:, lanes] * scale_in + o
            inten = jnp.exp(lin)
            ll_own[:, out_lanes] += jnp.sum((t * lin - inten).reshape(64, 8, 128), axis=0)
            res[h, rows, lanes] = (t - inten).astype(BF16)

    def matmul2(h, s):
        for i, k in enumerate(SCORE_STEPS[s]):
            part = jnp.dot(rect[zs[k]].reshape(256, n_rec), res[h], preferred_element_type=F32)
            scf[h, k] = part.reshape(NY, 2, 32, half)
            snd_c[h, s, i] = scf[h, k, :, 1 - c].astype(BF16)
        send(snd_c.at[h, s], rcv_c.at[h, s], c_r.at[h, s], sib)

    def y_send(h, k):
        for j in (2, 1, 3):
            send(snd_y.at[h, k, ys[j]], rcv_y.at[h, k, j], y_r.at[h, k], at(z, ys[j], c))

    def chip_sum(h, s):
        arrived(rcv_c.at[h, s], c_r.at[h, s])
        for i, k in enumerate(SCORE_STEPS[s]):
            total = scf[h, k, :, c] + rcv_c[h, s, i].astype(F32)
            if k in NEAR:
                snd_n[h, k // 7] = total.astype(BF16)
                send(snd_n.at[h, k // 7], rcv_n.at[h, k // 7], n_r.at[h], at(zs[k], y, c))
            else:
                scf[h, k, :, 0] = total
                if k:
                    snd_y[h, k] = total.astype(BF16)
                    y_send(h, k)

    def near_sum(h):
        total = scf[h, 0, :, 0]
        arrived(rcv_n.at[h], n_r.at[h])
        for i in range(2):
            total = total + rcv_n[h, i].astype(F32)
        scf[h, 0, :, 0] = total
        snd_y[h, 0] = total.astype(BF16)
        y_send(h, 0)

    def y_sum(h, k):
        total = scf[h, k, y, 0]
        arrived(rcv_y.at[h, k, pl.ds(0, 3)], y_r.at[h, k])
        for j in (1, 3, 2):
            total = total + rcv_y[h, k, j].astype(F32)
        return total

    def far_send(h, k):
        snd_z[h, k] = y_sum(h, k).astype(BF16)
        send(snd_z.at[h, k], rcv_z.at[h, k], z_r.at[h], at(zs[k], y, c))

    def z_sum(h):
        score = y_sum(h, 0)
        arrived(rcv_z.at[h, pl.ds(0, 5)], z_r.at[h])
        for k in FAR:
            score = score + rcv_z[h, k].astype(F32)
        scx[h, x] = score.astype(BF16)
        for k in (2, 1, 3):
            send(scx.at[h, x], scx.at[h, x], x_r.at[h], (xs[k], dp), x_sent)

    def resampled_score(h):
        arrived(scx.at[h, pl.ds(0, 3)], x_r.at[h])
        scores = jnp.concatenate([scx[h, q] for q in range(NX)], axis=1)
        return jnp.dot(scores, sel[:, h].reshape(NX * half, n_part), preferred_element_type=F32)

    for k in NEAR:
        to_sib(0, k)
    to_sib(1, 0)
    offs = offs_v[...].astype(F32)
    upper = (lax.broadcasted_iota(jnp.int32, (128, 128), 0) <= lax.broadcasted_iota(jnp.int32, (128, 128), 1)).astype(F32).astype(BF16)
    within = jnp.dot(offs.astype(BF16), upper, preferred_element_type=F32)
    slots = jnp.concatenate([slot_v[pl.ds(x * 4 + q, 1), :] for q in range(4)], axis=1).astype(F32)
    before = jnp.zeros((1, 1), F32)
    for i in range(offs.shape[0]):
        upto = within[i : i + 1, :] + before
        start = upto - offs[i : i + 1, :]
        upto_b = jnp.broadcast_to(upto, (128, 128)).T
        start_b = jnp.broadcast_to(start, (128, 128)).T
        for q in range(4):
            lanes = slice(128 * q, 128 * q + 128)
            hit = (slots[:, lanes] >= start_b) & (slots[:, lanes] < upto_b)
            sel[i // 4, (i % 4) // 2, 128 * (i % 2) : 128 * (i % 2) + 128, lanes] = jnp.where(hit, 1.0, 0.0).astype(BF16)
        before = before + within[i : i + 1, 127:128]

    arrived(thx.at[pl.ds(0, 3)], tx_r)
    everyone = jnp.concatenate([thx[q] for q in range(NX)], axis=1)
    hi = everyone.astype(BF16)
    rest = everyone - hi.astype(F32)
    mid = rest.astype(BF16)
    lo = (rest - mid.astype(F32)).astype(BF16)
    taken = jnp.dot(jnp.concatenate([hi, mid, lo], axis=0), sel[...].reshape(NX * n_part, n_part), preferred_element_type=F32)
    taken = taken[0:32] + taken[32:64] + taken[64:96]
    step = step_s[0]
    root = jnp.sqrt(jnp.full((1, 1), step, F32))
    acc[...] = (1.0 - 0.5 * step) * taken + root * nz_v[...]
    gain = 0.5 * step * tlev_s[0] * (temper_scale * scale_in)

    gathered(0)
    for i in range(4):
        matmul1(0, i)
    for k in FAR + NEAR:
        to_sib(1, k)
    for i in range(4):
        matmul2(0, i)
        if i > 1:
            chip_sum(0, i - 2)
    gathered(1)
    for i in range(4):
        matmul1(1, i)
        if i == 0:
            chip_sum(0, 2)
            chip_sum(0, 3)
    ll_rows[0] = jnp.sum(ll_own[...], axis=0, keepdims=True)
    send(ll_rows.at[0], ll_rows.at[1], lc_r, sib)
    for i in range(4):
        matmul2(1, i)
        if i > 1:
            chip_sum(1, i - 2)
        if i == 1:
            arrived(ll_rows.at[1], lc_r)
            ll_rows[2 + y] = ll_rows[0] + ll_rows[1]
            for k in (2, 1, 3):
                send(ll_rows.at[2 + y], ll_rows.at[2 + y], ly_r, at(z, ys[k], c))
    chip_sum(1, 2)
    chip_sum(1, 3)
    arrived(ll_rows.at[pl.ds(2, 3)], ly_r)
    ll_rows[6 + z] = (ll_rows[2] + ll_rows[3]) + (ll_rows[4] + ll_rows[5])
    for k in FAR + NEAR:
        send(ll_rows.at[6 + z], ll_rows.at[6 + z], lz_r, at(zs[k], y, c))
    near_sum(0)
    for k in (4, 3, 5, 2, 6):
        far_send(0, k)
    near_sum(1)
    for k in (4, 3, 5, 2, 6):
        far_send(1, k)
    arrived(ll_rows.at[pl.ds(6, 7)], lz_r)
    rows = [ll_rows[6 + q] for q in range(NZ)]
    ll_rows[14 + x] = ((rows[0] + rows[1]) + (rows[2] + rows[3])) + ((rows[4] + rows[5]) + (rows[6] + rows[7]))
    for k in (2, 1, 3):
        send(ll_rows.at[14 + x], ll_rows.at[14 + x], lx_r, (xs[k], dp))
    z_sum(0)
    acc[...] += gain * resampled_score(0)
    z_sum(1)

    arrived(ll_rows.at[pl.ds(14, 3)], lx_r)
    loglik = jnp.concatenate([ll_rows[14 + q] for q in range(NX)], axis=0)
    log_weight = tstep_s[0] * temper_scale * loglik
    peak = jnp.max(log_weight, axis=(0, 1), keepdims=True)
    shifted = jnp.exp(log_weight - peak)
    weight_sum = jnp.sum(shifted, axis=(0, 1), keepdims=True)
    weight_square = jnp.sum(shifted * shifted, axis=(0, 1), keepdims=True)
    le_ref[...] = peak + jnp.log(weight_sum) - math.log(NX * n_part)
    ess_ref[...] = weight_sum * weight_sum / (weight_square * (NX * n_part))

    out_ref[...] = acc[...] + gain * resampled_score(1)

    part = scx.at[:, pl.ds(0, 3)]
    pltpu.make_async_remote_copy(src_ref=part, dst_ref=part, send_sem=x_sent, recv_sem=x_sent, device_id=sib, device_id_type=MESH).wait_send()
    rows_sent = ll_rows.at[pl.ds(0, 14)]
    pltpu.make_async_remote_copy(src_ref=rows_sent, dst_ref=rows_sent, send_sem=row_sent, recv_sem=row_sent, device_id=sib, device_id_type=MESH).wait_send()
    assert sum(sends) % (32 * n_feat) == 0
    everything = rec.at[pl.ds(0, sum(sends) // (2 * n_feat))]
    pltpu.make_async_remote_copy(src_ref=everything, dst_ref=everything, send_sem=sent, recv_sem=sent, device_id=sib, device_id_type=MESH).wait_send()


def hand_over(*refs):
    for i in range(3):
        refs[3 + i][...] = refs[i][...]


def on_device(records, counts_obs, exposure_bin, bin_offset, theta, noise, offspring, slot_order, temper_step, temper_level, step_size):
    n_rec, n_feat = records.shape
    n_part, cols = theta.shape
    half = n_part // NH
    vmem, anywhere = pl.BlockSpec(memory_space=pltpu.VMEM), pl.BlockSpec(memory_space=pl.ANY)
    dma = pltpu.SemaphoreType.DMA
    counts_obs, exposure_bin, offspring, slot_order = (a.reshape(-1, 128) for a in (counts_obs, exposure_bin, offspring, slot_order))
    scratch = [
        pltpu.VMEM((n_rec, n_feat), BF16),
        pltpu.VMEM((NZ, NY, 64, n_rec), BF16),
        pltpu.VMEM((NH, NZ, NY, 2, cols, half), BF16),
        pltpu.VMEM((NH, n_rec, half), BF16),
        pltpu.VMEM((n_rec, 128), F32),
        pltpu.VMEM((n_rec, 128), F32),
        pltpu.VMEM((NX, NH, half, n_part), BF16),
        pltpu.VMEM((NX, cols, n_part), F32),
        pltpu.VMEM((cols, n_part), F32),
        pltpu.VMEM((NH, NZ, NY, 2, cols, half), F32),
        pltpu.VMEM((NH, 4, 2, NY, cols, half), BF16),
        pltpu.VMEM((NH, 4, 2, NY, cols, half), BF16),
        pltpu.VMEM((NH, 2, NY, cols, half), BF16),
        pltpu.VMEM((NH, 2, NY, cols, half), BF16),
        pltpu.VMEM((NH, NZ, NY, cols, half), BF16),
        pltpu.VMEM((NH, NZ, NY, cols, half), BF16),
        pltpu.VMEM((NH, NZ, cols, half), BF16),
        pltpu.VMEM((NH, NZ, cols, half), BF16),
        pltpu.VMEM((NH, NX, cols, half), BF16),
        pltpu.VMEM((8, n_part), F32),
        pltpu.VMEM((2 + NY + NZ + NX, 1, n_part), F32),
        pltpu.VMEM(counts_obs.shape, jnp.int32),
        pltpu.VMEM(exposure_bin.shape, jnp.int32),
        pltpu.VMEM((cols, n_part), F32),
        pltpu.VMEM((cols, n_part), F32),
        pltpu.VMEM(offspring.shape, jnp.int32),
        pltpu.VMEM(slot_order.shape, jnp.int32),
        pltpu.SMEM(bin_offset.shape, F32),
        pltpu.SMEM((1,), F32), pltpu.SMEM((1,), F32), pltpu.SMEM((1,), F32),
        dma((4,)), dma((10,)), dma, dma, dma,
        dma((NH, NZ)), dma((NH, NZ)), dma((NH,)), dma,
        dma((NH, 4)), dma((NH,)), dma((NH, NZ)), dma((NH,)), dma((NH,)),
        dma, dma, dma, dma,
    ]
    shapes = (
        jax.ShapeDtypeStruct((cols, n_part), F32),
        jax.ShapeDtypeStruct((1, 1), F32),
        jax.ShapeDtypeStruct((1, 1), F32),
    )
    results = pl.pallas_call(
        kernel,
        out_shape=shapes,
        in_specs=[anywhere] * 11,
        out_specs=(vmem, vmem, vmem),
        scratch_shapes=scratch,
        compiler_params=pltpu.CompilerParams(collective_id=0, has_side_effects=True, vmem_limit_bytes=60 << 20),
        cost_estimate=pl.CostEstimate(flops=4 * n_rec * n_feat * n_part, bytes_accessed=2 * n_rec * n_feat, transcendentals=n_rec * n_part),
    )(
        records, counts_obs, exposure_bin, bin_offset, theta.T, noise.T, offspring, slot_order,
        temper_step.reshape(1), temper_level.reshape(1), step_size.reshape(1),
    )
    moved, le, ess = pl.pallas_call(
        hand_over,
        out_shape=shapes,
        in_specs=[vmem] * 3,
        out_specs=(vmem,) * 3,
    )(*results)
    return moved.T, le[0, 0], ess[0, 0]


def solution(mesh):
    in_specs = (P("dp", None), P("dp"), P("dp"), P(), P("dom", "dp"), P("dom", "dp"), P(), P(), P(), P(), P())
    out_specs = (P("dom", "dp"), P(), P())
    return jax.shard_map(on_device, mesh=mesh, in_specs=in_specs, out_specs=out_specs, check_vma=False)
```
